128 devices in a mesh: pipe: 4 (over x), dp: 4 (over y_hi, core), tensor: 8 (over z, y_lo).
Axes of the slice: x: 4, y: 4 (y_hi: 2, y_lo: 2; y = y_hi * 2 + y_lo), z: 4, core: 2. Of those that a mesh axis runs over, the one named last changes fastest.
Arguments:
- activations: bfloat16 [4, 4, 1024, 8192], P('pipe', 'dp', None, 'tensor'), may hold values from -6 to 6
- analysis: bfloat16 [4, 8192, 2048], P('pipe', 'tensor'), may hold values from -0.0625 to 0.0625
- synthesis: bfloat16 [4, 2048, 8192], P('pipe', None, 'tensor'), may hold values from -0.125 to 0.125
- norm_gain: float32 [4, 8192], P('pipe'), may hold values from 0.1 to 1.9
- query_weight: bfloat16 [4, 8192, 4096], P('pipe', None, 'tensor'), may hold values from -4 to 4
- keys_values: bfloat16 [4, 8192, 2048], P('pipe', None, 'tensor'), may hold values from -1 to 1
- latent_grad: bfloat16 [4, 4, 1024, 2048], P('pipe', 'dp', 'tensor'), may hold values from -6 to 6
Outputs:
- attended: bfloat16 [4, 4, 1024, 4096], P('pipe', 'dp', None, 'tensor')
- activation_grad: bfloat16 [4, 4, 1024, 8192], P('pipe', 'dp', None, 'tensor')
The draws below stay inside these ranges and needn't reach their ends.
All inputs are finite; a program needn't handle non-finite values.
Results may differ from the reference program's by a relative error of at most 0.017.
Values may be sent and summed in bfloat16 or wider, within the bound.
A program may use at most 192 MiB of HBM per device.

```python
import jax
import jax.numpy as jnp
from jax import lax

D = 8192
KVH = 8
HEAD = 128
QH = 32
LAT = 2048
LEN = 1024
SECTIONS = 4
SEQS = 4


def shared_keys(key):
    return jax.random.normal(key, (SECTIONS, D, KVH, 2, HEAD), jnp.float32) * D ** (-0.5)


def draw_keys_values(key, part):
    shared = shared_keys(key)
    key = jax.random.fold_in(key, 5)
    spread = jnp.exp(jax.random.uniform(key, (SECTIONS, 1, KVH, 2, 1), jnp.float32, -0.3, 0.3))
    return jnp.clip(shared * spread, -1.0, 1.0).reshape(SECTIONS, D, KVH * 2 * HEAD).astype(jnp.bfloat16)


def draw_query_weight(key, part):
    key = jax.random.fold_in(key, 9)
    own_key = jax.random.fold_in(key, 0)
    own = jax.random.normal(own_key, (SECTIONS, D, KVH, QH // KVH, HEAD), jnp.float32) * D ** (-0.5)
    return jnp.clip(own, -4.0, 4.0).reshape(SECTIONS, D, QH * HEAD).astype(jnp.bfloat16)


def levels(key, dims, cuts, low, top_value):
    def one(position, parts):
        heights = jax.random.uniform(jax.random.fold_in(jax.random.fold_in(key, 6), position), (parts,), jnp.float32, low / len(cuts), top_value / len(cuts))
        return jnp.repeat(jnp.exp(heights), dims[position] // parts).reshape((-1,) + (1,) * (len(dims) - position - 1))

    loudness = one(*cuts[0])
    for cut in cuts[1:]:
        loudness = loudness * one(*cut)
    return loudness


def centred(key, dims, scale, limit, pieces=(), kind=jnp.bfloat16):
    drawn = jax.random.normal(key, dims, jnp.float32) * scale
    if len(pieces) > 0:
        drawn = levels(key, dims, pieces, -0.22, 0.18) * drawn
    return jnp.clip(drawn, min=-limit, max=limit).astype(kind)


def setup_inputs(seed: int = 0) -> dict:
    streams_of = jax.random.split(jax.random.key(seed), 8)
    activations = centred(streams_of[0], (SECTIONS, SEQS, LEN, D), 1.0, 6.0, ((0, 4), (1, 4), (3, 8)))
    analysis = centred(streams_of[1], (SECTIONS, D, LAT), D ** -0.5, 0.0625, ((0, 4), (1, 8)))
    synthesis = centred(streams_of[2], (SECTIONS, LAT, D), LAT ** -0.5, 0.125, ((0, 4), (2, 8)))
    norm_gain = jnp.clip(1.0 + 0.18 * jax.random.normal(streams_of[3], (SECTIONS, D), jnp.float32), 0.1, 1.9)
    query_weight = draw_query_weight(jax.random.fold_in(streams_of[7], 71), 0)
    keys_values = draw_keys_values(jax.random.fold_in(streams_of[7], 71), 0)
    latent_grad = centred(streams_of[6], (SECTIONS, SEQS, LEN, LAT), 1.0, 6.0, ((0, 4), (1, 4), (2, 8)))
    return {"activations": activations, "analysis": analysis, "synthesis": synthesis, "norm_gain": norm_gain, "query_weight": query_weight, "keys_values": keys_values, "latent_grad": latent_grad}


EPSILON = 1e-05
ROPE_BASE = 500000.0

def rotary(inputs, positions):
    half_width = inputs.shape[-1] // 2
    frequency = ROPE_BASE ** (-(jnp.arange(half_width, dtype=jnp.float32) * 2.0 / inputs.shape[-1]))
    angles = positions[:, None] * frequency[None, :]
    cosine = jnp.cos(angles)[:, None, :]
    sine_table = jnp.sin(angles)[:, None, :]
    leading = inputs[..., :half_width]
    trailing = inputs[..., half_width:]
    return jnp.concatenate([leading * cosine - trailing * sine_table, trailing * cosine + leading * sine_table], axis=-1)

def attend(queries, rotated_keys, values_in, anchor):
    row_count = queries.shape[0]
    scores = jnp.einsum('qkgd,skd->kgqs', queries.astype(jnp.float32), rotated_keys.astype(jnp.float32)) * HEAD ** (-0.5)
    row_pos = anchor + jnp.arange(row_count, dtype=jnp.int32)
    col_pos = jnp.arange(rotated_keys.shape[0], dtype=jnp.int32)
    visible = col_pos[None, :] <= row_pos[:, None]
    scores = jnp.where(visible[None, None], scores, -1e+30)
    maximum = lax.optimization_barrier(jnp.max(scores, axis=-1, keepdims=True))
    exponent = jnp.exp(scores - maximum)
    weights = (exponent / lax.optimization_barrier(jnp.sum(exponent, axis=-1, keepdims=True))).astype(jnp.bfloat16)
    mixed_values = jnp.einsum('kgqs,skd->qkgd', weights.astype(jnp.float32), values_in.astype(jnp.float32))
    return mixed_values.astype(jnp.bfloat16).reshape(row_count, -1)

def one_section(received, w_synth, gain, w_query, w_keyval):
    synthesized = jnp.dot(received.reshape(-1, LAT), w_synth, preferred_element_type=jnp.float32).astype(jnp.bfloat16)
    synth_float = synthesized.astype(jnp.float32)
    mean_square = lax.optimization_barrier(jnp.mean(synth_float * synth_float, axis=1, keepdims=True))
    normed = (synth_float * lax.rsqrt(mean_square + EPSILON) * gain[None, :]).astype(jnp.bfloat16)
    queries_all = jnp.dot(normed, w_query, preferred_element_type=jnp.float32)
    keyvals_all = jnp.dot(normed, w_keyval, preferred_element_type=jnp.float32)
    positions = jnp.arange(LEN, dtype=jnp.float32)

    def per_sequence(inputs):
        query_rows, keyval_rows = inputs
        queries = rotary(query_rows.reshape(LEN, QH, HEAD), positions).astype(jnp.bfloat16)
        queries = queries.reshape(LEN, KVH, QH // KVH, HEAD)
        key_value = keyval_rows.reshape(LEN, KVH, 2, HEAD)
        rotated_keys = rotary(key_value[:, :, 0], positions).astype(jnp.bfloat16)
        values_in = key_value[:, :, 1].astype(jnp.bfloat16)
        return attend(queries, rotated_keys, values_in, 0)
    return lax.map(per_sequence, (queries_all.reshape(SEQS, LEN, -1), keyvals_all.reshape(SEQS, LEN, -1)))

def reference(activations, analysis, synthesis, norm_gain, query_weight, keys_values, latent_grad):
    latents = []
    for section_index in range(SECTIONS):
        coded = jnp.dot(activations[section_index].reshape(-1, D), analysis[section_index], preferred_element_type=jnp.float32)
        latents.append(coded.astype(jnp.bfloat16).reshape(SEQS, LEN, LAT))
    attended = []
    gradients = []
    for section_index in range(SECTIONS):
        source = (section_index - 1) % SECTIONS
        attended.append(one_section(latents[source], synthesis[section_index], norm_gain[section_index], query_weight[section_index], keys_values[section_index]))
        later = (section_index + 1) % SECTIONS
        back = lax.dot_general(latent_grad[later].reshape(-1, LAT), analysis[section_index], (((1,), (1,)), ((), ())), preferred_element_type=jnp.float32)
        gradients.append(back.astype(jnp.bfloat16).reshape(SEQS, LEN, D))
    return (jnp.stack(attended), jnp.stack(gradients))
```

```python
import functools

import jax
import jax.numpy as jnp
import numpy as np
from jax import lax
from jax.experimental import pallas as pl
from jax.experimental.pallas import tpu as pltpu
from jax.sharding import PartitionSpec as P

D = 8192
HEAD = 128
LAT = 2048
LEN = 1024
FEAT = 1024
EPSILON = 1e-05
ROPE_BASE = 500000.0
MESH = pl.DeviceIdType.MESH

RA = 48
RB = 128 - RA
N_IN = 128
N_OUT = 512 - N_IN
HALF = LAT // 2
N_COPIES = 104
BF = jnp.bfloat16
F32 = jnp.float32


def dot(a, b):
    return jnp.dot(a, b, preferred_element_type=F32)


def dot_t(a, b):
    return lax.dot_general(a, b, (((1,), (1,)), ((), ())), preferred_element_type=F32)


def rotated(u, cosine, sine):
    return u * cosine + pltpu.roll(u, HEAD // 2, 1) * sine


def kernel(
    acts_h, ana_h, syn_h, gain_h, wq_h, wkv_h, lg_h, cos_h, sin_h,
    att_h, grad_h,
    acts, ana, syn, gain, wq, wkv, cos, sin,
    part, lat, gl, sg, wp, wacc,
    ya, fb0, fb1, nb0, nb1, fa0, fa1, na0, na1, yb,
    ssv, ssall,
    lsem, ssem, rsem,
):
    p = lax.axis_index("pipe")
    dp = lax.axis_index("dp")
    t = lax.axis_index("tensor")
    z, yl = t // 2, t % 2
    yh, core = dp // 2, dp % 2
    oy = 1 - yl
    zf, zp, zm = (z + 2) % 4, (z + 1) % 4, (z + 3) % 4

    up = (p, dp, zp * 2 + yl)
    down = (p, dp, zm * 2 + yl)
    side = (p, dp, z * 2 + oy)
    outer = (p, (1 - yh) * 2 + core, z * 2 + oy)
    later = ((p + 1) % 4, dp, t)
    before = ((p + 3) % 4, dp, t)
    mate = (p, yh * 2 + 1 - core, t)
    across = (p, (1 - yh) * 2 + core, t)
    peers = [(p, dp, (t + i) % 8) for i in range(1, 8)]

    def rows_a(zz, y):
        return pl.ds(pl.multiple_of(zz * 256 + y * RA, 16), RA)

    def rows_b(zz, y):
        return pl.ds(pl.multiple_of(zz * 256 + 2 * RA + y * RB, 16), RB)

    def rows_bb(zz):
        return pl.ds(pl.multiple_of(zz * 256 + 2 * RA, 16), 2 * RB)

    def chunk(zz):
        return pl.ds(pl.multiple_of(zz * 256, 256), 256)

    lo, hi = pl.ds(0, HALF), pl.ds(HALF, HALF)

    key_cols, value_cols = pl.ds(512, HEAD), pl.ds(512 + HEAD, HEAD)

    def kv_at(zz):
        rows = pl.ds(pl.multiple_of(zz % 2 * 256, 256), 256)
        return rows, pl.ds(pl.multiple_of(zz // 2 * 256, 256), 128), pl.ds(pl.multiple_of(zz // 2 * 256 + 128, 128), 128)

    remote = []

    def send(src, dst, device):
        i = len(remote)
        copy = pltpu.make_async_remote_copy(
            src_ref=src, dst_ref=dst, send_sem=ssem.at[i], recv_sem=rsem.at[i],
            device_id=device, device_id_type=MESH,
        )
        copy.start()
        remote.append(copy)
        return copy

    n_local = [0]

    def local(src, dst):
        copy = pltpu.make_async_copy(src, dst, lsem.at[n_local[0]])
        n_local[0] += 1
        copy.start()
        return copy

    l_acts = local(acts_h, acts)
    l_ana = local(ana_h, ana)
    l_gain = local(gain_h, gain)
    l_syn = local(syn_h, syn)

    barrier = pltpu.get_barrier_semaphore()
    friends = peers + [outer, later, before, mate, across]
    for device in friends:
        pl.semaphore_signal(barrier, inc=1, device_id=device, device_id_type=MESH)
    pl.semaphore_wait(barrier, len(friends))

    g_shift_b = send(lg_h.at[pl.ds(RA, RB)], gl.at[rows_b(z, yl)], before)
    g_shift_a = send(lg_h.at[pl.ds(0, RA)], gl.at[rows_a(z, yl)], before)

    def encode(zz):
        @pl.loop(0, LAT // 512)
        def _(n):
            cols = pl.ds(pl.multiple_of(n * 512, 512), 512)
            part[chunk(zz), cols] = dot(acts[chunk(zz), :], ana[:, cols]).astype(BF)

    def fuse(k, first=False):
        rows = pl.ds(pl.multiple_of(k * FEAT, FEAT), FEAT)

        def add(cols, value):
            if first:
                wacc[:, cols] = value
            else:
                wacc[:, cols] += value

        @pl.loop(0, 2)
        def _(n):
            cols = pl.ds(pl.multiple_of(n * 256, 256), 256)
            add(cols, dot(sg[k], wq[rows, cols]))

        add(pl.ds(512, 256), dot(sg[k], wkv[rows, :]))

    eye = lax.broadcasted_iota(jnp.int32, (128, 128), 0) == lax.broadcasted_iota(jnp.int32, (128, 128), 1)

    def squares(zz):
        def step(n, total):
            cols = pl.ds(pl.multiple_of(n * 256, 256), 256)
            y = dot(lat[chunk(zz), :], syn[:, cols]).astype(BF).astype(F32)
            y = y * y
            return total + y[:, :128] + y[:, 128:]

        total = lax.fori_loop(0, FEAT // 256, step, jnp.zeros((256, 128), F32))
        column = jnp.sum(total, axis=1, keepdims=True)
        for i in range(2):
            ssv[zz * 2 + i] = jnp.sum(
                jnp.where(eye, column[i * 128:(i + 1) * 128], 0.0), axis=0, keepdims=True
            )

    def project(zz):
        rows = chunk(zz)

        @pl.loop(0, 2)
        def _(n):
            cols = pl.ds(pl.multiple_of(n * 256, 256), 256)
            y = dot(lat[rows, :], wp[:, cols])
            c, s = cos[rows, :], sin[rows, :]
            y = jnp.concatenate([rotated(y[:, :128], c, s), rotated(y[:, 128:], c, s)], axis=1)
            acts[rows, cols] = y.astype(BF)

        y = dot(lat[rows, :], wp[:, 512:768])
        kv_rows, k_cols, v_cols = kv_at(zz)
        wacc[kv_rows, k_cols] = rotated(y[:, :128], cos[rows, :], sin[rows, :])
        wacc[kv_rows, v_cols] = y[:, 128:]

    def scale_keys():
        @pl.loop(0, 4)
        def _(zz):
            kv_rows, k_cols, v_cols = kv_at(zz)
            for i in range(2):
                total = ssall[0, zz * 2 + i]
                for source in range(1, 8):
                    total = total + ssall[source, zz * 2 + i]
                scale = lax.rsqrt(total * (1.0 / D) + EPSILON)
                column = jnp.sum(jnp.where(eye, scale, 0.0), axis=1, keepdims=True)
                rows = pl.ds(pl.multiple_of(zz * 256 + i * 128, 128), 128)
                here = pl.ds(pl.multiple_of(zz % 2 * 256 + i * 128, 128), 128)
                acts[rows, key_cols] = (wacc[here, k_cols] * column).astype(BF)
                acts[rows, value_cols] = (wacc[here, v_cols] * column).astype(BF)
                s_cols = pl.ds(pl.multiple_of(512 + zz // 2 * 128, 128), 128)
                wacc[here, s_cols] = jnp.broadcast_to(column * HEAD ** (-0.5), (128, 128))

    def attend(h):
        cols = pl.ds(h * HEAD, HEAD)
        for i in range(4):
            end = 256 * (i + 1)
            rows = pl.ds(256 * i, 256)
            scores = dot_t(acts[rows, cols], acts[:end, key_cols])
            row = lax.broadcasted_iota(jnp.int32, (256, end), 0) + 256 * i
            col = lax.broadcasted_iota(jnp.int32, (256, end), 1)
            scores = jnp.where(col <= row, scores, -1e30)
            top = jnp.max(scores, axis=1, keepdims=True)
            factor = wacc[pl.ds(i % 2 * 256, 256), pl.ds(512 + i // 2 * 128, 1)]
            weights = jnp.exp((scores - top) * factor)
            total = jnp.sum(weights, axis=1, keepdims=True)
            mixed = dot(weights.astype(BF), acts[:end, value_cols])
            acts[rows, cols] = (mixed / total).astype(BF)

    outs = []

    def gradient(zz):
        @pl.loop(0, FEAT // 256)
        def _(n):
            cols = pl.ds(pl.multiple_of(n * 256, 256), 256)
            part[chunk(zz), cols] = dot_t(gl[chunk(zz), :], ana[cols, :]).astype(BF)

        for y in range(2):
            for src, off, size in ((rows_a(zz, y), 0, RA), (rows_b(zz, y), RA, RB)):
                dst = pl.ds(pl.multiple_of(zz * 256 + y * 128 + off, 16), size)
                outs.append(local(part.at[src, pl.ds(0, FEAT)], grad_h.at[dst, :]))

    def gather(x, own_a, own_b):
        own_b.wait_recv()
        b = rows_b(z, yl)
        b_side = send(x.at[b], x.at[b], side)
        b_up = send(x.at[b], x.at[b], up)
        b_down = send(x.at[b], x.at[b], down)
        own_a.wait_recv()
        a = rows_a(z, yl)
        a_up = send(x.at[a], x.at[a], up)
        a_down = send(x.at[a], x.at[a], down)
        a_side = [send(x.at[a], x.at[a], side)]
        yield
        b_side.wait_recv()
        b = rows_b(z, oy)
        c_up = send(x.at[b], x.at[b], up)
        c_down = send(x.at[b], x.at[b], down)
        yield
        a_up.wait_recv()
        a = rows_a(zm, yl)
        a_far0 = send(x.at[a, lo], x.at[a, lo], up)
        a_side.append(send(x.at[a], x.at[a], side))
        a_down.wait_recv()
        a = rows_a(zp, yl)
        a_far1 = send(x.at[a, hi], x.at[a, hi], down)
        a_side.append(send(x.at[a], x.at[a], side))
        yield
        b_up.wait_recv()
        c_up.wait_recv()
        b = rows_bb(zm)
        b_far0 = send(x.at[b, lo], x.at[b, lo], up)
        b_down.wait_recv()
        c_down.wait_recv()
        b = rows_bb(zp)
        b_far1 = send(x.at[b, hi], x.at[b, hi], down)
        yield
        a_far0.wait_recv()
        a_far1.wait_recv()
        a = rows_a(zf, yl)
        a_side.append(send(x.at[a], x.at[a], side))
        a_side[0].wait_recv()
        yield
        a_side[1].wait_recv()
        yield
        a_side[2].wait_recv()
        yield
        b_far0.wait_recv()
        b_far1.wait_recv()
        a_side[3].wait_recv()
        yield

    l_acts.wait()
    l_ana.wait()
    l_wq = local(wq_h, wq)
    l_wkv = local(wkv_h, wkv)
    l_cos = local(cos_h, cos)
    l_sin = local(sin_h, sin)
    encode(zf)
    bf_up = send(part.at[rows_bb(zf), lo], fb0, up)
    bf_down = send(part.at[rows_bb(zf), hi], fb1, down)
    y_a = [send(part.at[rows_a(zf, oy)], ya.at[0], side)]
    encode(zp)
    bn_up1 = send(part.at[rows_bb(zp), hi], nb0.at[:, hi], up)
    y_a.append(send(part.at[rows_a(zp, oy)], ya.at[1], side))
    encode(zm)
    bn_down0 = send(part.at[rows_bb(zm), lo], nb1.at[:, lo], down)
    y_a.append(send(part.at[rows_a(zm, oy)], ya.at[2], side))
    encode(z)
    y_a.append(send(part.at[rows_a(z, oy)], ya.at[3], side))

    l_gain.wait()
    l_syn.wait()
    in_start = pl.multiple_of(yh * (LAT - 2 * N_IN) + core * N_IN, 16)
    out_start = pl.multiple_of(jnp.where(yh == yl, 2 * N_IN, LAT // 2) + core * N_OUT, 16)
    scale = gain[:, pl.ds(pl.multiple_of(t * FEAT, FEAT), FEAT)]
    sg[t, :N_IN, :] = (syn[pl.ds(in_start, N_IN), :].astype(F32) * scale).astype(BF)
    sg[t, N_IN:, :] = (syn[pl.ds(out_start, N_OUT), :].astype(F32) * scale).astype(BF)

    near, far_half = pl.ds(0, N_IN), pl.ds(N_IN, N_OUT)

    def spread(k):
        return (
            send(sg.at[k, near], sg.at[k, near], side),
            send(sg.at[k, far_half], sg.at[k, far_half], outer),
        )

    s_up = send(sg.at[t], sg.at[t], up)
    s_down = send(sg.at[t], sg.at[t], down)
    s_own = spread(t)
    l_wq.wait()
    l_wkv.wait()
    fuse(t, first=True)

    bf_up.wait_recv()
    part[rows_bb(zp), lo] = part[rows_bb(zp), lo] + fb0[...]
    bn_up0 = send(part.at[rows_bb(zp), lo], nb0.at[:, lo], up)
    bf_down.wait_recv()
    part[rows_bb(zm), hi] = part[rows_bb(zm), hi] + fb1[...]
    bn_down1 = send(part.at[rows_bb(zm), hi], nb1.at[:, hi], down)

    def add_side(i, zz):
        y_a[i].wait_recv()
        part[rows_a(zz, yl), :] = part[rows_a(zz, yl), :] + ya[i]

    add_side(0, zf)
    af_up = send(part.at[rows_a(zf, yl), lo], fa0, up)
    af_down = send(part.at[rows_a(zf, yl), hi], fa1, down)
    add_side(1, zp)
    an_up1 = send(part.at[rows_a(zp, yl), hi], na0.at[:, hi], up)
    add_side(2, zm)
    an_down0 = send(part.at[rows_a(zm, yl), lo], na1.at[:, lo], down)
    add_side(3, z)

    for copy in (bn_up1, bn_down0, bn_up0, bn_down1):
        copy.wait_recv()

    def sum_b(y):
        here = pl.ds(pl.multiple_of(y * RB, 16), RB)
        return part[rows_b(z, y), :].astype(F32) + nb0[here, :].astype(F32) + nb1[here, :].astype(F32)

    part[rows_b(z, oy), :] = sum_b(oy).astype(BF)
    b_side = send(part.at[rows_b(z, oy)], yb, side)

    af_up.wait_recv()
    part[rows_a(zp, yl), lo] = part[rows_a(zp, yl), lo] + fa0[...]
    an_up0 = send(part.at[rows_a(zp, yl), lo], na0.at[:, lo], up)
    af_down.wait_recv()
    part[rows_a(zm, yl), hi] = part[rows_a(zm, yl), hi] + fa1[...]
    an_down1 = send(part.at[rows_a(zm, yl), hi], na1.at[:, hi], down)

    quarter0, quarter1 = pl.ds(0, FEAT // 2), pl.ds(FEAT // 2, FEAT // 2)
    s_up.wait_recv()
    k = zm * 2 + yl
    sf_up = send(sg.at[k, :, quarter0], sg.at[k, :, quarter0], up)
    s_m = spread(k)
    s_down.wait_recv()
    k = zp * 2 + yl
    sf_down = send(sg.at[k, :, quarter1], sg.at[k, :, quarter1], down)
    s_p = spread(k)

    b_side.wait_recv()
    part[rows_b(z, yl), :] = (sum_b(yl) + yb[...].astype(F32)).astype(BF)
    r_shift_b = send(part.at[rows_b(z, yl)], lat.at[rows_b(z, yl)], later)
    for copy in (an_up1, an_down0, an_up0, an_down1):
        copy.wait_recv()
    part[rows_a(z, yl), :] = (
        part[rows_a(z, yl), :].astype(F32) + na0[...].astype(F32) + na1[...].astype(F32)
    ).astype(BF)
    r_shift_a = send(part.at[rows_a(z, yl)], lat.at[rows_a(z, yl)], later)

    fuse(zm * 2 + yl)
    fuse(zp * 2 + yl)
    sf_up.wait_recv()
    sf_down.wait_recv()
    s_f = spread(zf * 2 + yl)

    gather_l = gather(lat, r_shift_a, r_shift_b)
    gather_g = gather(gl, g_shift_a, g_shift_b)
    next(gather_l)
    next(gather_g)
    fuse(zf * 2 + yl)
    for copies, zz in ((s_own, z), (s_m, zm), (s_p, zp)):
        for copy in copies:
            copy.wait_recv()
        fuse(zz * 2 + oy)
    next(gather_l)
    next(gather_g)
    for copy in s_f:
        copy.wait_recv()
    fuse(zf * 2 + oy)

    mine = (pl.ds(in_start, N_IN), pl.ds(out_start, N_OUT))
    wp[mine[0], :] = wacc[:N_IN, :].astype(BF)
    wp[mine[1], :] = wacc[N_IN:, :].astype(BF)
    w_mate = [send(wp.at[rows], wp.at[rows], mate) for rows in mine]
    w_across = [send(wp.at[rows], wp.at[rows], across) for rows in mine]
    next(gather_l)
    next(gather_l)
    next(gather_g)
    next(gather_g)
    for copy in w_across:
        copy.wait_recv()
    a_in = pl.multiple_of((1 - yh) * (LAT - 2 * N_IN) + core * N_IN, 16)
    a_out = pl.multiple_of(jnp.where(yh != yl, 2 * N_IN, LAT // 2) + core * N_OUT, 16)
    theirs = (pl.ds(a_in, N_IN), pl.ds(a_out, N_OUT))
    w_relay = [send(wp.at[rows], wp.at[rows], mate) for rows in theirs]
    next(gather_l)
    squares(z)
    next(gather_l)
    squares(zm)
    next(gather_l)
    squares(zp)
    for copy in w_mate + w_relay:
        copy.wait_recv()
    l_cos.wait()
    l_sin.wait()
    project(z)
    project(zm)
    project(zp)
    next(gather_g)
    next(gather_l)
    squares(zf)
    ssall[t] = ssv[...]
    ss_copies = [send(ssv, ssall.at[t], device) for device in peers]
    project(zf)
    for copy in ss_copies:
        copy.wait_recv()
    scale_keys()

    for h in range(4):
        attend(h)
    l_att = local(acts.at[:, pl.ds(0, 512)], att_h)
    for copy in remote:
        copy.wait_send()
    gradient(z)
    next(gather_g)
    gradient(zm)
    next(gather_g)
    gradient(zp)
    next(gather_g)
    gradient(zf)
    l_att.wait()
    for copy in outs:
        copy.wait()


def tables():
    frequency = ROPE_BASE ** (-(np.arange(HEAD // 2) * 2.0 / HEAD))
    angles = np.arange(LEN)[:, None] * frequency[None, :]
    cosine, sine = np.cos(angles), np.sin(angles)
    return (
        np.concatenate([cosine, cosine], axis=1).astype(np.float32),
        np.concatenate([-sine, sine], axis=1).astype(np.float32),
    )


def on_device(activations, analysis, synthesis, norm_gain, query_weight, keys_values, latent_grad):
    cos, sin = tables()
    anywhere = pl.BlockSpec(memory_space=pl.ANY)

    def vmem(*shape, dtype=BF):
        return pltpu.VMEM(shape, dtype)

    attended, grad = pl.pallas_call(
        kernel,
        out_shape=(
            jax.ShapeDtypeStruct((LEN, 512), BF),
            jax.ShapeDtypeStruct((LEN, FEAT), BF),
        ),
        in_specs=[anywhere] * 9,
        out_specs=(anywhere, anywhere),
        scratch_shapes=[
            vmem(LEN, FEAT), vmem(FEAT, LAT), vmem(LAT, FEAT), vmem(1, D, dtype=F32),
            vmem(D, 512), vmem(D, 256), vmem(LEN, HEAD, dtype=F32), vmem(LEN, HEAD, dtype=F32),
            vmem(LEN, LAT), vmem(LEN, LAT), vmem(LEN, LAT), vmem(8, 512, FEAT), vmem(LAT, 768),
            vmem(512, 768, dtype=F32),
            vmem(4, RA, LAT), vmem(2 * RB, HALF), vmem(2 * RB, HALF), vmem(2 * RB, LAT), vmem(2 * RB, LAT),
            vmem(RA, HALF), vmem(RA, HALF), vmem(RA, LAT), vmem(RA, LAT),
            vmem(RB, LAT),
            vmem(8, 1, 128, dtype=F32), vmem(8, 8, 1, 128, dtype=F32),
            pltpu.SemaphoreType.DMA((32,)),
            pltpu.SemaphoreType.DMA((N_COPIES,)),
            pltpu.SemaphoreType.DMA((N_COPIES,)),
        ],
        compiler_params=pltpu.CompilerParams(
            collective_id=0, has_side_effects=True, vmem_limit_bytes=63 * 2**20
        ),
        cost_estimate=pl.CostEstimate(flops=28 * 10**9, bytes_accessed=30 * 10**6, transcendentals=0),
    )(
        activations[0, 0], analysis[0], synthesis[0], norm_gain, query_weight[0], keys_values[0],
        latent_grad[0, 0], jnp.asarray(cos), jnp.asarray(sin),
    )
    return attended[None, None], grad[None, None]


def solution(mesh):
    return jax.shard_map(
        on_device,
        mesh=mesh,
        in_specs=(
            P("pipe", "dp", None, "tensor"),
            P("pipe", "tensor", None),
            P("pipe", None, "tensor"),
            P("pipe", None),
            P("pipe", None, "tensor"),
            P("pipe", None, "tensor"),
            P("pipe", "dp", "tensor", None),
        ),
        out_specs=(P("pipe", "dp", None, "tensor"), P("pipe", "dp", None, "tensor")),
        check_vma=False,
    )
```

```python
import functools

import jax
import jax.numpy as jnp
import numpy as np
from jax import lax
from jax.experimental import pallas as pl
from jax.experimental.pallas import tpu as pltpu
from jax.sharding import PartitionSpec as P

D = 8192
HEAD = 128
LAT = 2048
LEN = 1024
FEAT = 1024
EPSILON = 1e-05
LOG2_E = 1.4426950408889634
ROPE_BASE = 500000.0
MESH = pl.DeviceIdType.MESH

RA = 48
RB = 128 - RA
RG = 48
N_IN = 128
N_OUT = 512 - N_IN


def pieces_of():
    out = []
    for q in range(4):
        cut = min(max(N_IN, q * 128), q * 128 + 128)
        parts = [("in", q * 128, cut - q * 128), ("out", cut, q * 128 + 128 - cut)]
        out.append(tuple(part for part in parts if part[2]))
    return tuple(out)


PIECES = pieces_of()
HALF = LAT // 2
N_COPIES = 144
BF = jnp.bfloat16
F32 = jnp.float32


def dot(a, b):
    return jnp.dot(a, b, preferred_element_type=F32)


def dot_t(a, b):
    return lax.dot_general(a, b, (((1,), (1,)), ((), ())), preferred_element_type=F32)


def rotated(u, cosine, sine):
    return u * cosine + pltpu.roll(u, HEAD // 2, 1) * sine


ORDER = [
    16, 31, 15, 41, 17, 0, 56, 1, 24, 2, 27, 36, 22, 20, 5, 4, 3, 35, 6, 19, 7, 9, 8, 21, 45, 29, 12, 28, 18, 10,
    11, 47, 49, 34, 26, 25, 50, 38, 23, 14, 13, 30, 75, 32, 33, 42, 48, 60, 68, 40, 39, 67, 43, 37, 57, 51, 70, 59,
    71, 46, 69, 44, 61, 62, 58, 52, 53, 63, 64, 74, 83, 76, 72, 73, 86, 77, 54, 89, 65, 55, 66, 92, 95, 79, 90, 84,
    78, 87, 93, 80, 81, 85, 96, 99, 103, 104, 82, 102, 98, 101, 97, 100, 88, 105, 91, 94,
]


class Names:
    def __getattr__(self, name):
        return name


K = Names()


def join(*parts):
    return "".join(str(part) for part in parts)


def kernel(
    acts_h, ana_h, syn_h, gain_h, wq_h, wkv_h, lg_h, cos_h, sin_h,
    att_h, grad_h,
    acts, ana, syn, gain, wq, wkv, cos, sin,
    part, lat, gl, sg, wp, wacc,
    ya, fb0, fb1, nb0, nb1, fa0, fa1, na0, na1, yb,
    ssv, ssall,
    lsem, ssem, rsem,
):
    p = lax.axis_index("pipe")
    dp = lax.axis_index("dp")
    t = lax.axis_index("tensor")
    z, yl = t // 2, t % 2
    yh, core = dp // 2, dp % 2
    oy = 1 - yl
    at_z = {"o": z, "p": (z + 1) % 4, "m": (z + 3) % 4, "f": (z + 2) % 4}

    up = (p, dp, at_z["p"] * 2 + yl)
    down = (p, dp, at_z["m"] * 2 + yl)
    side = (p, dp, z * 2 + oy)
    outer = (p, (1 - yh) * 2 + core, z * 2 + oy)
    later = ((p + 1) % 4, dp, t)
    before = ((p + 3) % 4, dp, t)
    mate = (p, yh * 2 + 1 - core, t)
    across = (p, (1 - yh) * 2 + core, t)
    peers = [(p, dp, (t + i) % 8) for i in range(1, 8)]

    def rows_a(zz, y, ra=RA):
        return pl.ds(pl.multiple_of(zz * 256 + y * ra, 16), ra)

    def rows_b(zz, y, ra=RA):
        return pl.ds(pl.multiple_of(zz * 256 + 2 * ra + y * (128 - ra), 16), 128 - ra)

    def rows_bb(zz, ra=RA):
        return pl.ds(pl.multiple_of(zz * 256 + 2 * ra, 16), 256 - 2 * ra)

    def chunk(zz):
        return pl.ds(pl.multiple_of(zz * 256, 256), 256)

    lo, hi = pl.ds(0, HALF), pl.ds(HALF, HALF)

    key_cols, value_cols = pl.ds(512, HEAD), pl.ds(512 + HEAD, HEAD)

    def kv_at(zz):
        rows = pl.ds(pl.multiple_of(zz % 2 * 256, 256), 256)
        cols = zz // 2 * 256
        return rows, pl.ds(pl.multiple_of(cols, 256), 128), pl.ds(pl.multiple_of(cols + 128, 128), 128)

    remote = {}
    arrived = set()

    def send(name, src, dst, device):
        i = len(remote)
        copy = pltpu.make_async_remote_copy(
            src_ref=src, dst_ref=dst, send_sem=ssem.at[i], recv_sem=rsem.at[i],
            device_id=device, device_id_type=MESH,
        )
        copy.start()
        remote[name] = copy

    def arrive(name):
        if name not in arrived:
            arrived.add(name)
            remote[name].wait_recv()

    local_copies = {}

    def local(name, src, dst):
        copy = pltpu.make_async_copy(src, dst, lsem.at[len(local_copies)])
        copy.start()
        local_copies[name] = copy

    def loaded(name):
        if name not in arrived:
            arrived.add(name)
            local_copies[name].wait()

    def encode(zz):
        @pl.loop(0, LAT // 512, unroll=True)
        def _(n):
            cols = pl.ds(pl.multiple_of(n * 512, 512), 512)
            part[chunk(zz), cols] = dot(acts[chunk(zz), :], ana[:, cols]).astype(BF)

    started = []

    def fuse(k, j):
        rows = pl.ds(pl.multiple_of(k * FEAT, FEAT), FEAT)
        here = pl.ds(j * 256, 256)

        def add(cols, value):
            if j not in started:
                wacc[here, cols] = value
            else:
                wacc[here, cols] += value

        @pl.loop(0, 2, unroll=True)
        def _(n):
            cols = pl.ds(pl.multiple_of(n * 256, 256), 256)
            add(cols, dot(sg[k, here, :], wq[rows, cols]))

        add(pl.ds(512, 256), dot(sg[k, here, :], wkv[rows, :]))

    def diagonal():
        return lax.broadcasted_iota(jnp.int32, (128, 128), 0) == lax.broadcasted_iota(jnp.int32, (128, 128), 1)

    def squares(zz):
        def step(n, total):
            cols = pl.ds(pl.multiple_of(n * 256, 256), 256)
            y = dot(lat[chunk(zz), :], syn[:, cols]).astype(BF).astype(F32)
            y = y * y
            return total + y[:, :128] + y[:, 128:]

        total = lax.fori_loop(0, FEAT // 256, step, jnp.zeros((256, 128), F32), unroll=True)
        column = jnp.sum(total, axis=1, keepdims=True)
        for i in range(2):
            ssv[zz * 2 + i] = jnp.sum(
                jnp.where(diagonal(), column[i * 128:(i + 1) * 128], 0.0), axis=0, keepdims=True
            )

    def project(zz):
        rows = chunk(zz)

        @pl.loop(0, 2, unroll=True)
        def _(n):
            cols = pl.ds(pl.multiple_of(n * 256, 256), 256)
            y = dot(lat[rows, :], wp[:, cols])
            c, s = cos[rows, :], sin[rows, :]
            y = jnp.concatenate([rotated(y[:, :128], c, s), rotated(y[:, 128:], c, s)], axis=1)
            acts[rows, cols] = y.astype(BF)

        y = dot(lat[rows, :], wp[:, 512:768])
        kv_rows, k_cols, v_cols = kv_at(zz)
        wacc[kv_rows, k_cols] = rotated(y[:, :128], cos[rows, :], sin[rows, :])
        wacc[kv_rows, v_cols] = y[:, 128:]

    def scale_keys():
        @pl.loop(0, 4)
        def _(zz):
            kv_rows, k_cols, v_cols = kv_at(zz)
            for i in range(2):
                total = ssall[0, zz * 2 + i]
                for source in range(1, 8):
                    total = total + ssall[source, zz * 2 + i]
                scale = lax.rsqrt(total * (1.0 / D) + EPSILON)
                column = jnp.sum(jnp.where(diagonal(), scale, 0.0), axis=1, keepdims=True)
                rows = pl.ds(pl.multiple_of(zz * 256 + i * 128, 128), 128)
                here = pl.ds(pl.multiple_of(zz % 2 * 256 + i * 128, 128), 128)
                acts[rows, key_cols] = (wacc[here, k_cols] * column).astype(BF)
                acts[rows, value_cols] = (wacc[here, v_cols] * column).astype(BF)
                s_cols = pl.ds(pl.multiple_of(512 + zz // 2 * 128, 128), 128)
                wacc[here, s_cols] = jnp.broadcast_to(column * (HEAD ** (-0.5) * LOG2_E), (128, 128))

    def attend(h, blocks):
        cols = pl.ds(h * HEAD, HEAD)
        for i in blocks:
            end = 256 * (i + 1)
            rows = pl.ds(256 * i, 256)
            scores = dot_t(acts[rows, cols], acts[:end, key_cols])
            row = lax.broadcasted_iota(jnp.int32, (256, end), 0) + 256 * i
            col = lax.broadcasted_iota(jnp.int32, (256, end), 1)
            scores = jnp.where(col <= row, scores, -1e30)
            top = jnp.max(scores, axis=1, keepdims=True)
            factor = wacc[pl.ds(i % 2 * 256, 256), pl.ds(512 + i // 2 * 128, 1)]
            weights = jnp.exp2((scores - top) * factor)
            total = jnp.sum(weights, axis=1, keepdims=True)
            mixed = dot(weights.astype(BF), acts[:end, value_cols])
            acts[rows, cols] = (mixed / total).astype(BF)

    def gradient(zz):
        @pl.loop(0, FEAT // 256, unroll=True)
        def _(n):
            cols = pl.ds(pl.multiple_of(n * 256, 256), 256)
            part[chunk(zz), cols] = dot_t(gl[chunk(zz), :], ana[cols, :]).astype(BF)

    steps = {}

    def step(name, copies=(), after=(), kind=""):
        def register(body):
            steps[name] = (tuple(copies), tuple(after), kind, body)
            return body

        return register

    @step(K.enc_f)
    def _():
        loaded(K.acts)
        loaded(K.ana)
        local(K.wq, wq_h, wq)
        local(K.wkv, wkv_h, wkv)
        local(K.cos, cos_h, cos)
        local(K.sin, sin_h, sin)
        encode(at_z["f"])
        send(K.bf_up, part.at[rows_bb(at_z["f"]), lo], fb0, up)
        send(K.bf_dn, part.at[rows_bb(at_z["f"]), hi], fb1, down)
        send(K.ya_f, part.at[rows_a(at_z["f"], oy)], ya.at[0], side)

    @step(K.enc_p, after=[K.enc_f])
    def _():
        encode(at_z["p"])
        send(K.bn_up1, part.at[rows_bb(at_z["p"]), hi], nb0.at[:, hi], up)
        send(K.ya_p, part.at[rows_a(at_z["p"], oy)], ya.at[1], side)

    @step(K.enc_m, after=[K.enc_p])
    def _():
        encode(at_z["m"])
        send(K.bn_dn0, part.at[rows_bb(at_z["m"]), lo], nb1.at[:, lo], down)
        send(K.ya_m, part.at[rows_a(at_z["m"], oy)], ya.at[2], side)

    @step(K.enc_o, after=[K.enc_m])
    def _():
        encode(at_z["o"])
        send(K.ya_o, part.at[rows_a(at_z["o"], oy)], ya.at[3], side)

    @step(K.rb_up, [K.bf_up], [K.enc_p])
    def _():
        here = (rows_bb(at_z["p"]), lo)
        part[here] = part[here] + fb0[...]
        send(K.bn_up0, part.at[here], nb0.at[:, lo], up)

    @step(K.rb_dn, [K.bf_dn], [K.enc_m])
    def _():
        here = (rows_bb(at_z["m"]), hi)
        part[here] = part[here] + fb1[...]
        send(K.bn_dn1, part.at[here], nb1.at[:, hi], down)

    def add_side(i, w):
        here = rows_a(at_z[w], yl)
        part[here, :] = part[here, :] + ya[i]

    @step(K.ra_f, [K.ya_f], [K.enc_f])
    def _():
        add_side(0, "f")
        send(K.af_up, part.at[rows_a(at_z["f"], yl), lo], fa0, up)
        send(K.af_dn, part.at[rows_a(at_z["f"], yl), hi], fa1, down)

    @step(K.ra_p, [K.ya_p], [K.enc_p])
    def _():
        add_side(1, "p")
        send(K.an_up1, part.at[rows_a(at_z["p"], yl), hi], na0.at[:, hi], up)

    @step(K.ra_m, [K.ya_m], [K.enc_m])
    def _():
        add_side(2, "m")
        send(K.an_dn0, part.at[rows_a(at_z["m"], yl), lo], na1.at[:, lo], down)

    @step(K.ra_o, [K.ya_o], [K.enc_o])
    def _():
        add_side(3, "o")

    @step(K.ra_up, [K.af_up], [K.ra_p])
    def _():
        here = (rows_a(at_z["p"], yl), lo)
        part[here] = part[here] + fa0[...]
        send(K.an_up0, part.at[here], na0.at[:, lo], up)

    @step(K.ra_dn, [K.af_dn], [K.ra_m])
    def _():
        here = (rows_a(at_z["m"], yl), hi)
        part[here] = part[here] + fa1[...]
        send(K.an_dn1, part.at[here], na1.at[:, hi], down)

    def sum_b(y):
        here = pl.ds(pl.multiple_of(y * RB, 16), RB)
        return part[rows_b(z, y), :].astype(F32) + nb0[here, :].astype(F32) + nb1[here, :].astype(F32)

    @step(K.b_sum, [K.bn_up0, K.bn_up1, K.bn_dn0, K.bn_dn1], [K.enc_o])
    def _():
        part[rows_b(z, oy), :] = sum_b(oy).astype(BF)
        send(K.yb, part.at[rows_b(z, oy)], yb, side)

    @step(K.b_red, [K.yb], [K.b_sum])
    def _():
        part[rows_b(z, yl), :] = (sum_b(yl) + yb[...].astype(F32)).astype(BF)
        send(K.l_shift_b, part.at[rows_b(z, yl)], lat.at[rows_b(z, yl)], later)

    @step(K.a_red, [K.an_up0, K.an_up1, K.an_dn0, K.an_dn1], [K.ra_o])
    def _():
        part[rows_a(z, yl), :] = (
            part[rows_a(z, yl), :].astype(F32) + na0[...].astype(F32) + na1[...].astype(F32)
        ).astype(BF)
        send(K.l_shift_a, part.at[rows_a(z, yl)], lat.at[rows_a(z, yl)], later)

    def place(segment, group):
        kind, first, size = segment
        if kind == "in":
            at = group * (LAT - 2 * N_IN) + core * N_IN + first
        else:
            at = (N_IN * 2 + (group + yl) % 2 * (LAT // 2 - 2 * N_IN)) + core * N_OUT + first - N_IN
        return pl.multiple_of(at, 16)

    def scale_step(j):
        @step(join(K.s_scale, j), kind="s")
        def _():
            loaded(K.gain)
            loaded(K.syn)
            scale = gain[:, pl.ds(pl.multiple_of(t * FEAT, FEAT), FEAT)]
            for q in (2 * j, 2 * j + 1):
                for segment in PIECES[q]:
                    _, first, size = segment
                    rows = pl.ds(place(segment, yh), size)
                    sg[t, pl.ds(first, size), :] = (syn[rows, :].astype(F32) * scale).astype(BF)

    def column(w):
        return at_z[w] * 2 + yl

    quarters = pl.ds(0, FEAT // 2), pl.ds(FEAT // 2, FEAT // 2)

    sources = {"o": [], "m": [K.s_up], "p": [K.s_dn], "f": [K.s_far_up, K.s_far_dn]}
    earlier = {"o": [K.s_scale], "m": [K.s_z], "p": [K.s_z], "f": [K.s_fu, K.s_fd]}

    def fill(names, q):
        return [join(name, q // 2 if name == K.s_scale else q) for name in names]

    def synthesis_steps(q):
        rows = pl.ds(q * 128, 128)

        @step(join(K.s_z, q), after=[join(K.s_scale, q // 2)], kind="s")
        def _():
            send(join(K.s_up, q), sg.at[t, rows], sg.at[t, rows], up)
            send(join(K.s_dn, q), sg.at[t, rows], sg.at[t, rows], down)

        @step(join(K.s_fu, q), [join(K.s_up, q)], [join(K.s_z, q)], kind="s")
        def _():
            k = column("m")
            send(join(K.s_far_up, q), sg.at[k, rows, quarters[0]], sg.at[k, rows, quarters[0]], up)

        @step(join(K.s_fd, q), [join(K.s_dn, q)], [join(K.s_z, q)], kind="s")
        def _():
            k = column("p")
            send(join(K.s_far_dn, q), sg.at[k, rows, quarters[1]], sg.at[k, rows, quarters[1]], down)

        for w in "ompf":
            for kind, first, size in PIECES[q]:
                def spread(w=w, kind=kind, first=first, size=size):
                    ref = sg.at[column(w), pl.ds(first, size)]
                    send(join(K.s_, kind, "_", w, q), ref, ref, side if kind == "in" else outer)

                step(join(K.s_y, kind, "_", w, q), fill(sources[w], q), fill(earlier[w], q), kind="s")(spread)

    def fuse_steps(j):
        both = (2 * j, 2 * j + 1)

        def fuse_into(k):
            loaded(K.wq)
            loaded(K.wkv)
            fuse(k, j)
            started.append(j)

        for w in "ompf":
            def own(w=w):
                fuse_into(column(w))

            def others(w=w):
                fuse_into(at_z[w] * 2 + oy)

            copies = [name for q in both for name in fill(sources[w], q)]
            after = [name for q in both for name in fill(earlier[w], q)]
            step(join(K.u_, w, j), copies, [K.enc_f] + after, kind=K.fuse)(own)
            parts = [join(part[0], "_", w, q) for q in both for part in PIECES[q]]
            step(
                join(K.t_, w, j), [K.s_ + part for part in parts], [K.enc_f] + [K.s_y + part for part in parts], kind=K.fuse
            )(others)

        @step(join(K.w_out, j), after=[join(u, w, j) for u in (K.u_, K.t_) for w in "ompf"])
        def _():
            for q in both:
                for segment in PIECES[q]:
                    kind, first, size = segment
                    mine = pl.ds(place(segment, yh), size)
                    wp[mine, :] = wacc[first:first + size, :].astype(BF)
                    send(join(K.w_across, kind, q), wp.at[mine], wp.at[mine], across)
                    send(join(K.w_mate, kind, q), wp.at[mine], wp.at[mine], mate)

        for q in both:
            for segment in PIECES[q]:
                def relay(q=q, segment=segment):
                    theirs = pl.ds(place(segment, 1 - yh), segment[2])
                    send(join(K.w_last, segment[0], q), wp.at[theirs], wp.at[theirs], mate)

                step(join(K.w_relay, segment[0], q), [join(K.w_across, segment[0], q)], [join(K.w_out, j)])(relay)

    for j in range(2):
        scale_step(j)
    for q in range(4):
        synthesis_steps(q)
    for j in range(2):
        fuse_steps(j)

    fused = [join(part[0], q) for q in range(4) for part in PIECES[q]]

    def gather_steps(g, x, first, ra):
        def pass_on(name, where, device, cols=None):
            ref = x.at[where] if cols is None else x.at[where, cols]
            send(g + name, ref, ref, device)

        @step(g + K.b0, [g + K.shift_b], first, kind=g)
        def _():
            here = rows_b(z, yl, ra)
            pass_on(K.b_side, here, side)
            pass_on(K.b_up, here, up)
            pass_on(K.b_dn, here, down)

        @step(g + K.a0, [g + K.shift_a], first, kind=g)
        def _():
            here = rows_a(z, yl, ra)
            pass_on(K.a_up, here, up)
            pass_on(K.a_dn, here, down)
            pass_on(K.a_side_o, here, side)

        @step(g + K.b1, [g + K.b_side], [g + K.b0], kind=g)
        def _():
            here = rows_b(z, oy, ra)
            pass_on(K.c_up, here, up)
            pass_on(K.c_dn, here, down)

        @step(g + K.am, [g + K.a_up], [g + K.a0], kind=g)
        def _():
            here = rows_a(at_z["m"], yl, ra)
            pass_on(K.a_far_up, here, up, lo)
            pass_on(K.a_side_m, here, side)

        @step(g + K.ap, [g + K.a_dn], [g + K.a0], kind=g)
        def _():
            here = rows_a(at_z["p"], yl, ra)
            pass_on(K.a_far_dn, here, down, hi)
            pass_on(K.a_side_p, here, side)

        @step(g + K.bm, [g + K.b_up, g + K.c_up], [g + K.b1], kind=g)
        def _():
            pass_on(K.b_far_up, rows_bb(at_z["m"], ra), up, lo)

        @step(g + K.bp, [g + K.b_dn, g + K.c_dn], [g + K.b1], kind=g)
        def _():
            pass_on(K.b_far_dn, rows_bb(at_z["p"], ra), down, hi)

        @step(g + K.af, [g + K.a_far_up, g + K.a_far_dn], [g + K.am, g + K.ap], kind=g)
        def _():
            pass_on(K.a_side_f, rows_a(at_z["f"], yl, ra), side)

    gather_steps(K.l_, lat, [K.a_red, K.b_red], RA)
    gather_steps(K.g_, gl, [], RG)

    def whole(g, w):
        copies, after = {
            "o": ([K.shift_a, K.shift_b, K.b_side, K.a_side_o], [K.b0, K.a0]),
            "m": ([K.b_up, K.c_up, K.a_up, K.a_side_m], [K.b1, K.am]),
            "p": ([K.b_dn, K.c_dn, K.a_dn, K.a_side_p], [K.b1, K.ap]),
            "f": ([K.b_far_up, K.b_far_dn, K.a_far_up, K.a_far_dn, K.a_side_f], [K.bm, K.bp, K.af]),
        }[w]
        return [g + name for name in copies], [g + name for name in after]

    def token_steps(w):
        copies, after = whole(K.l_, w)

        @step(K.sq_ + w, copies, after, kind=K.squares)
        def _():
            squares(at_z[w])

        @step(K.pr_ + w, copies + [c + i for c in (K.w_mate, K.w_last) for i in fused],
              after + [K.w_relay + i for i in fused], kind=K.project)
        def _():
            loaded(K.cos)
            loaded(K.sin)
            project(at_z[w])

        copies, after = whole(K.g_, w)

        @step(K.gr_ + w, copies, after + [K.pr_ + u for u in "ompf"], kind=K.gradient)
        def _():
            if not flushed:
                flushed.append(w)
                for name in part_sends:
                    remote[name].wait_send()
            zz = at_z[w]
            gradient(zz)
            for y in range(2):
                for part_name, src, off, size in (("a", rows_a(zz, y, RG), 0, RG), ("b", rows_b(zz, y, RG), RG, 128 - RG)):
                    dst = pl.ds(pl.multiple_of(zz * 256 + y * 128 + off, 16), size)
                    local(join(K.out_, w, y, part_name), part.at[src, pl.ds(0, FEAT)], grad_h.at[dst, :])

    flushed = []
    part_sends = [
        K.bf_up, K.bf_dn, K.ya_f, K.bn_up1, K.ya_p, K.bn_dn0, K.ya_m, K.ya_o, K.bn_up0, K.bn_dn1, K.af_up, K.af_dn,
        K.an_up1, K.an_dn0, K.an_up0, K.an_dn1, K.yb, K.l_shift_b, K.l_shift_a,
    ]
    for w in "ompf":
        token_steps(w)

    ss_names = [join(K.ss, i) for i in range(7)]

    @step(K.ss, after=[K.sq_ + w for w in "ompf"])
    def _():
        ssall[t] = ssv[...]
        for name, device in zip(ss_names, peers):
            send(name, ssv, ssall.at[t], device)

    @step(K.keys, ss_names, [K.ss] + [K.pr_ + w for w in "ompf"], kind=K.keys)
    def _():
        scale_keys()

    def attend_step(h, j):
        @step(join(K.at_, h, j), after=[K.keys], kind=K.attend)
        def _():
            attend(h, ((0, 3), (1, 2))[j])

    for h in range(4):
        for j in range(2):
            attend_step(h, j)

    @step(K.att, after=[join(K.at_, h, j) for h in range(4) for j in range(2)], kind=K.attend)
    def _():
        local(K.att, acts.at[:, pl.ds(0, 512)], att_h)

    local(K.acts, acts_h, acts)
    local(K.ana, ana_h, ana)
    local(K.gain, gain_h, gain)
    local(K.syn, syn_h, syn)

    barrier = pltpu.get_barrier_semaphore()
    friends = peers + [outer, later, before, mate, across]
    for device in friends:
        pl.semaphore_signal(barrier, inc=1, device_id=device, device_id_type=MESH)
    pl.semaphore_wait(barrier, len(friends))

    send(K.g_shift_b, lg_h.at[pl.ds(RG, 128 - RG)], gl.at[rows_b(z, yl, RG)], before)
    send(K.g_shift_a, lg_h.at[pl.ds(0, RG)], gl.at[rows_a(z, yl, RG)], before)

    done = set()
    names = list(steps)
    for name in [names[i] for i in ORDER]:
        copies, after, _, body = steps[name]
        if not done.issuperset(after):
            raise ValueError(name)
        for copy in copies:
            arrive(copy)
        body()
        done.add(name)
    if done != set(steps):
        raise ValueError(sorted(set(steps) - done))

    for name in remote:
        if name not in arrived:
            arrive(name)
        if name not in part_sends:
            remote[name].wait_send()
    for name in local_copies:
        loaded(name)


def tables():
    frequency = ROPE_BASE ** (-(np.arange(HEAD // 2) * 2.0 / HEAD))
    angles = np.arange(LEN)[:, None] * frequency[None, :]
    cosine, sine = np.cos(angles), np.sin(angles)
    return (
        np.concatenate([cosine, cosine], axis=1).astype(np.float32),
        np.concatenate([-sine, sine], axis=1).astype(np.float32),
    )


def emit_kernel(att, grad, att_out, grad_out):
    att_out[...] = att[...]
    grad_out[...] = grad[...]


def on_device(activations, analysis, synthesis, norm_gain, query_weight, keys_values, latent_grad):
    cos, sin = tables()
    anywhere = pl.BlockSpec(memory_space=pl.ANY)

    def vmem(*shape, dtype=BF):
        return pltpu.VMEM(shape, dtype)

    shapes = (jax.ShapeDtypeStruct((LEN, 512), BF), jax.ShapeDtypeStruct((LEN, FEAT), BF))
    attended, grad = pl.pallas_call(
        kernel,
        out_shape=shapes,
        in_specs=[anywhere] * 9,
        out_specs=(anywhere, anywhere),
        scratch_shapes=[
            vmem(LEN, FEAT), vmem(FEAT, LAT), vmem(LAT, FEAT), vmem(1, D, dtype=F32),
            vmem(D, 512), vmem(D, 256), vmem(LEN, HEAD, dtype=F32), vmem(LEN, HEAD, dtype=F32),
            vmem(LEN, LAT), vmem(LEN, LAT), vmem(LEN, LAT), vmem(8, 512, FEAT), vmem(LAT, 768),
            vmem(512, 768, dtype=F32),
            vmem(4, RA, LAT), vmem(2 * RB, HALF), vmem(2 * RB, HALF), vmem(2 * RB, LAT), vmem(2 * RB, LAT),
            vmem(RA, HALF), vmem(RA, HALF), vmem(RA, LAT), vmem(RA, LAT),
            vmem(RB, LAT),
            vmem(8, 1, 128, dtype=F32), vmem(8, 8, 1, 128, dtype=F32),
            pltpu.SemaphoreType.DMA((32,)),
            pltpu.SemaphoreType.DMA((N_COPIES,)),
            pltpu.SemaphoreType.DMA((N_COPIES,)),
        ],
        compiler_params=pltpu.CompilerParams(
            collective_id=0, has_side_effects=True, vmem_limit_bytes=63 * 2**20
        ),
        cost_estimate=pl.CostEstimate(flops=28 * 10**9, bytes_accessed=30 * 10**6, transcendentals=0),
    )(
        activations[0, 0], analysis[0], synthesis[0], norm_gain, query_weight[0], keys_values[0],
        latent_grad[0, 0], jnp.asarray(cos), jnp.asarray(sin),
    )
    attended, grad = pl.pallas_call(
        emit_kernel,
        out_shape=shapes,
        grid=(4,),
        in_specs=[pl.BlockSpec((256, 512), lambda i: (i, 0)), pl.BlockSpec((256, FEAT), lambda i: (i, 0))],
        out_specs=(pl.BlockSpec((256, 512), lambda i: (i, 0)), pl.BlockSpec((256, FEAT), lambda i: (i, 0))),
    )(attended, grad)
    return attended[None, None], grad[None, None]


def solution(mesh):
    return jax.shard_map(
        on_device,
        mesh=mesh,
        in_specs=(
            P("pipe", "dp", None, "tensor"),
            P("pipe", "tensor", None),
            P("pipe", None, "tensor"),
            P("pipe", None),
            P("pipe", None, "tensor"),
            P("pipe", None, "tensor"),
            P("pipe", "dp", "tensor", None),
        ),
        out_specs=(P("pipe", "dp", None, "tensor"), P("pipe", "dp", None, "tensor")),
        check_vma=False,
    )
```
